32 devices in a mesh: groups: 1, ep: 16 (over z, y, x), sub: 2 (over core).
Axes of the slice: x: 2, y: 2, z: 4, core: 2. Of those that a mesh axis runs over, the one named last changes fastest.
Arguments:
- expert_inputs: bfloat16 [2, 512, 8, 768], P(None, ('groups', 'ep', 'sub')), may hold values from -6 to 6
- routes: int32 [2, 512, 8], P(None, ('groups', 'ep', 'sub')), may hold values from 0 to 15, all different within a row; in each aligned block of 16 rows (0 to 15, 16 to 31, ..., all dimensions but the last counted through in order) at most 16 rows name the same one
- route_weights: float32 [2, 512, 8], P(None, ('groups', 'ep', 'sub')), may hold values from 0.05 to 0.5
- master: float32 [16, 768, 2048], P('ep', 'sub'), as said below
- old_steps: float32 [16, 6, 2048], P('ep', 'sub'), as said below
- move_list: int32 [16, 4], replicated, may hold values from 0 to 15, as said below
Outputs:
- mixed: bfloat16 [2, 512, 2048], P(None, ('groups', 'ep', 'sub'))
- new_levels: bfloat16 [16, 768, 2048], P(('groups', 'ep'), 'sub')
- new_steps: float32 [16, 6, 2048], P(('groups', 'ep'), 'sub')
The draws below stay inside these ranges and needn't reach their ends.
Inputs may be any that keep to these rules, and one draw needn't show every extreme that they name: `routes`: in each step the 8 experts of a token differ, and in each aligned block of 16 tokens, the tokens of one device, no expert is named by more than 16 of them; some expert is named by exactly 16. `move_list`: every expert has one row; the old owners, and the new owners, each take every index of ep once; no expert keeps its owner; the expert that arrives at a device moves in the same step as the one that leaves it. `master`: in every block of 128 rows of one column, one entry has the largest magnitude m, and every entry lies within 0.3 m / 127 of a whole multiple of m / 127. `old_steps`: Positive.
All inputs are finite; a program needn't handle non-finite values.
Results may differ from the reference program's by a relative error of at most 0.0059.
Values may be sent and summed in bfloat16 or wider, within the bound.
A program may use at most 64 MiB of HBM per device.

```python
import math
import jax
import jax.numpy as jnp
import numpy as np
from jax import lax

D = 2048
INNER = 768
Q_BLOCK = 128
TOP = 8
STEPS = 2
TOK_DEV = 16
EXPERTS = 16
TOKENS = 512
CAP = 16
N_EP = 16
N_SUB = 2


def grid_factors(key):
    factor = jnp.exp(jax.random.uniform(key, (EXPERTS, INNER // Q_BLOCK, D), jnp.float32, math.log(0.35), math.log(2.8)))
    return factor / (36.0 * math.sqrt(INNER))


def draw_master(key, part):
    factors = grid_factors(key)
    key = jax.random.fold_in(key, 11)
    subkeys = jax.random.split(key, 4)
    block_count = INNER // Q_BLOCK
    shape_four = (EXPERTS, block_count, Q_BLOCK, D)
    whole = jax.random.randint(subkeys[0], shape_four, -126, 127)
    placed = jax.random.randint(subkeys[1], (EXPERTS, block_count, 1, D), 0, Q_BLOCK)
    signs = jax.random.randint(subkeys[2], (EXPERTS, block_count, 1, D), 0, 2) * 2 - 1
    peaks = jnp.arange(Q_BLOCK)[None, None, :, None] == placed
    whole = jnp.where(peaks, 127 * signs, whole)
    offsets = jnp.clip(0.12 * jax.random.normal(subkeys[3], shape_four, jnp.float32), -0.3, 0.3)
    offsets = jnp.where(peaks, 0.0, offsets)
    values = (whole.astype(jnp.float32) + offsets) * factors[:, :, None, :]
    return values.reshape(EXPERTS, INNER, D)


def draw_old_steps(key, part):
    factors = grid_factors(key)
    key = jax.random.fold_in(key, 12)
    ratios = jnp.exp(jax.random.uniform(key, factors.shape, jnp.float32, math.log(0.8), math.log(1.25)))
    return factors * ratios


def draw_move_list(key, part):
    key = jax.random.fold_in(key, 13)
    subkeys = jax.random.split(key, 3)
    owners = jax.random.permutation(subkeys[0], EXPERTS).astype(jnp.int32)
    device_order = jax.random.permutation(subkeys[1], EXPERTS).astype(jnp.int32)
    positions = jnp.argsort(device_order, stable=True).astype(jnp.int32)
    placed = positions[owners]
    classes = placed * STEPS // EXPERTS
    following = placed + 1
    same_class = (following < EXPERTS) & (following * STEPS // EXPERTS == classes)
    class_start = (classes * EXPERTS + STEPS - 1) // STEPS
    targets = jnp.where(same_class, following, class_start)
    new_owners = device_order[targets]
    experts = jnp.arange(EXPERTS, dtype=jnp.int32)
    table_rows = jnp.stack([experts, owners, new_owners, classes], axis=1)
    return table_rows[jax.random.permutation(subkeys[2], EXPERTS)].astype(jnp.int32)


def block_scale(own_key, extent, cuts, low, high):
    level, own = 1.0, jax.random.fold_in(own_key, 6)
    for position, blocks in cuts:
        draws = jnp.exp(jax.random.uniform(jax.random.fold_in(own, position), (blocks,), jnp.float32, low / len(cuts), high / len(cuts)))
        level = level * jnp.repeat(draws, extent[position] // blocks).reshape([-1 if axis == position else 1 for axis in range(len(extent))])
    return level


def routed_block(own_key, own, number, rows, count, top, most, lean):
    sequence = jax.random.permutation(own_key, count)
    heavy_load, ordinary = load_shares(count, rows * top, most, lean, True), load_shares(count, rows * top, most, lean, False)
    places = jnp.arange(count)

    def named(sizes, turn):
        used = int((sizes > 0).sum())
        fixed = max(1, used // 4)
        passed = fixed + (places - fixed + turn * (used - fixed)) % max(1, count - fixed)
        return jnp.zeros((count,), jnp.int32).at[sequence[jnp.where(places < fixed, places, passed)]].set(jnp.asarray(sizes, jnp.int32))

    sizes = jnp.where(number % 4 == 0, named(heavy_load, number // 4), named(ordinary, number - number // 4 - 1))
    mixed = jax.random.permutation(jax.random.fold_in(own, 3), count)
    source_of, sink = mixed[0:count // 2 * 2:2], mixed[1:count // 2 * 2:2]
    slack = jnp.minimum(sizes[source_of] - 1, most - sizes[sink]) // 2
    slack = jnp.where((source_of == sequence[0]) | (sink == sequence[0]) | (sizes[sink] == 0), 0, jnp.maximum(slack, 0))
    passed = jax.random.randint(jax.random.fold_in(own, 4), (count // 2,), 0, 1 << 20) % (slack + 1)
    sizes = sizes.at[source_of].add(-passed).at[sink].add(passed)
    items = jnp.searchsorted(jnp.cumsum(sizes), jnp.arange(rows * top), side="right").astype(jnp.int32)
    grid = items.reshape(top, rows).T
    grid = grid[jax.random.permutation(jax.random.fold_in(own, 1), rows)]
    turn = jax.random.randint(jax.random.fold_in(own, 2), (rows, 1), 0, top)
    return jnp.take_along_axis(grid, (jnp.arange(top)[None, :] + turn) % top, axis=1)


def load_shares(number_of, total, reach, slope, full):
    portions = [(1 << 20) // math.isqrt(standing ** slope) + 1 for standing in range(1, number_of + 1)]
    largest = reach if full else min(reach, max(-(-total // number_of), total * portions[0] // sum(portions)))
    least = 1 if total - largest >= number_of - 1 else 0
    given, rest = [largest] + [least] * (number_of - 1), total - largest - least * (number_of - 1)
    while rest > 0:
        free = [i for i in range(1, number_of) if given[i] < largest] or [i for i in range(1, number_of) if given[i] < reach]
        mass, budget = sum([portions[i] for i in free]), rest
        for i in free:
            addition = min(reach - given[i], max(1, budget * portions[i] // mass), rest)
            given[i] = given[i] + addition
            rest = rest - addition
    return np.array(given)


def scatter_about(stream_key, shape, spread, bound, cuts=(), kind=jnp.bfloat16):
    values = jax.random.normal(stream_key, shape, jnp.float32) * spread
    if len(cuts) > 0:
        values = block_scale(stream_key, shape, cuts, -0.22, 0.18) * values
    return jnp.clip(values, min=-bound, max=bound).astype(kind)


def setup_inputs(seed: int = 0, part: int = 0) -> dict:
    keys = jax.random.split(jax.random.key(seed), 7)
    part_keys = jax.random.split(jax.random.fold_in(keys[6], part), 7)
    expert_inputs = scatter_about(part_keys[0], (STEPS, TOKENS, TOP, INNER), 1.0, 6.0, ((1, 32),))
    routes_keys = jax.random.split(jax.random.fold_in(part_keys[1], 1), STEPS * TOKENS // TOK_DEV)
    routes_turns = jax.random.permutation(jax.random.fold_in(part_keys[1], 3), STEPS * TOKENS // TOK_DEV)
    routes = jax.vmap(lambda own, number: routed_block(jax.random.fold_in(part_keys[1], 2), own, number, TOK_DEV, EXPERTS, TOP, CAP, 2))(routes_keys, routes_turns).reshape((STEPS, TOKENS, TOP))
    route_weights = jnp.clip(jnp.exp(math.log(0.5) - 2.3025851 * jax.random.uniform(part_keys[2], (STEPS, TOKENS, TOP), jnp.float32) ** block_scale(part_keys[2], (STEPS, TOKENS, TOP), ((1, 32),), -0.2, 0.2)), 0.05, 0.5)
    master = draw_master(jax.random.fold_in(keys[6], 71), part)
    old_steps = draw_old_steps(jax.random.fold_in(keys[6], 71), part)
    move_list = draw_move_list(jax.random.fold_in(keys[6], 71), part)
    return dict(expert_inputs=expert_inputs, routes=routes, route_weights=route_weights, master=master, old_steps=old_steps, move_list=move_list)


EPSILON = 1e-6


def grid_of(weights):
    blocks = weights.reshape(INNER // Q_BLOCK, Q_BLOCK, D)
    return (jnp.max(jnp.abs(blocks), axis=1) + EPSILON) / 127.0


def levels_of(weights, step_grid):
    blocks = weights.reshape(INNER // Q_BLOCK, Q_BLOCK, D)
    nearest = jnp.floor(blocks / step_grid[:, None, :] + 0.5)
    return jnp.clip(nearest, -127.0, 127.0).reshape(INNER, D)


def reference(expert_inputs, routes, route_weights, master, old_steps, move_list):
    empty_table = jnp.zeros((EXPERTS,), jnp.int32)
    old_owner = empty_table.at[move_list[:, 0]].set(move_list[:, 1])
    move_step = empty_table.at[move_list[:, 0]].set(move_list[:, 3])
    arrive_from = empty_table.at[move_list[:, 2]].set(move_list[:, 1])

    def arrived_copy(source):
        weights = lax.dynamic_index_in_dim(master, source, 0, keepdims=False)
        step_grid = grid_of(weights)
        levels = levels_of(weights, step_grid)
        return (levels * 0.0078125).astype(jnp.bfloat16), step_grid

    new_levels, new_steps = lax.map(arrived_copy, arrive_from)

    max_rows = N_EP * N_SUB * CAP
    pair_count = TOKENS * TOP
    half_rows = INNER // 2
    results = []
    for step_index in range(STEPS):
        expert_ids = routes[step_index].reshape(-1).astype(jnp.int32)
        token_rows = expert_inputs[step_index].reshape(-1, INNER).astype(jnp.float32)
        sort_order = jnp.argsort(expert_ids, stable=True).astype(jnp.int32)
        sorted_rows = jnp.concatenate([token_rows[sort_order], jnp.zeros((max_rows, INNER), jnp.float32)], axis=0)
        matches = (expert_ids[:, None] == jnp.arange(EXPERTS, dtype=jnp.int32)[None, :]).astype(jnp.int32)
        counts = jnp.sum(matches, axis=0).astype(jnp.int32)
        starts = (jnp.cumsum(counts) - counts).astype(jnp.int32)

        def serve_one(outputs, expert):
            old_device = old_owner[expert]
            weights = lax.dynamic_index_in_dim(master, old_device, 0, keepdims=False)
            stale_grid = lax.dynamic_index_in_dim(old_steps, old_device, 0, keepdims=False)
            step_grid = jnp.where(move_step[expert] <= step_index, grid_of(weights), stale_grid)
            levels = levels_of(weights, step_grid)
            scaled = (levels.reshape(INNER // Q_BLOCK, Q_BLOCK, D) * step_grid[:, None, :]).reshape(INNER, D)
            slot_rows = lax.dynamic_slice_in_dim(sorted_rows, starts[expert], max_rows, 0)
            halves = []
            for part_index in range(2):
                first_row = part_index * half_rows
                running = jnp.dot(slot_rows[:, first_row:first_row + half_rows], scaled[first_row:first_row + half_rows], precision=lax.Precision.HIGHEST)
                halves.append(running.astype(jnp.bfloat16))
            joined = (halves[0].astype(jnp.float32) + halves[1].astype(jnp.float32)).astype(jnp.bfloat16)
            outputs = lax.dynamic_update_slice_in_dim(outputs, joined, starts[expert], 0)
            return outputs, None

        outputs, _ = lax.scan(serve_one, jnp.zeros((pair_count + max_rows, D), jnp.bfloat16), jnp.arange(EXPERTS, dtype=jnp.int32))
        expert_out = jnp.zeros((pair_count, D), jnp.bfloat16).at[sort_order].set(outputs[:pair_count])
        weighted = jnp.sum(route_weights[step_index][:, :, None] * expert_out.reshape(TOKENS, TOP, D).astype(jnp.float32), axis=1)
        results.append(weighted.astype(jnp.bfloat16))
    return jnp.stack(results), new_levels, new_steps
```

```python
import functools

import jax
import jax.numpy as jnp
from jax import lax
from jax.experimental import pallas as pl
from jax.experimental.pallas import tpu as pltpu
from jax.sharding import PartitionSpec as P

Q_BLOCK = 128


EPSILON = 1e-06


def grid_of(weights):
    blocks = weights.reshape(-1, Q_BLOCK, weights.shape[-1])
    return (jnp.max(jnp.abs(blocks), axis=1) + EPSILON) / 127.0


def levels_of(weights, step_grid):
    blocks = weights.reshape(step_grid.shape[0], Q_BLOCK, weights.shape[-1])
    nearest = jnp.floor(blocks / step_grid[:, None, :] + 0.5)
    return jnp.clip(nearest, -127.0, 127.0).reshape(weights.shape).astype(jnp.bfloat16)


def dequantize(levels, step_grid):
    blocks = levels.reshape(step_grid.shape[0], Q_BLOCK, levels.shape[-1]).astype(jnp.float32)
    return (blocks * step_grid[:, None, :]).reshape(levels.shape)


def lookup(key_column, value_column, queries):
    matches = key_column[None, :] == queries[:, None]
    return jnp.sum(jnp.where(matches, value_column[None, :], 0), axis=1)


def local(expert_inputs, routes, route_weights, master, old_steps, move_list):
    experts = lax.axis_size("ep")
    my_index = lax.axis_index("ep")
    step_count, token_count, top_count, inner_width = expert_inputs.shape
    half_width = master.shape[1]
    out_width = master.shape[2]
    capacity = min(token_count, max(2, 2 * token_count * top_count // experts))
    all_experts = jnp.arange(experts, dtype=jnp.int32)
    expert_column = move_list[:, 0]
    old_column = move_list[:, 1]
    new_column = move_list[:, 2]
    step_column = move_list[:, 3]
    old_owner = lookup(expert_column, old_column, all_experts)
    new_owner = lookup(expert_column, new_column, all_experts)
    move_step = lookup(expert_column, step_column, all_experts)
    arrive_from = lookup(new_column, old_column, all_experts)
    leave_step = lookup(old_column, step_column, jnp.reshape(my_index, (1,)))[0]
    own_master = master[0]
    stale_grid = old_steps[0]
    stale_levels = levels_of(own_master, stale_grid)
    spread = lax.all_to_all(
        own_master.reshape(experts, -1), "ep", split_axis=0, concat_axis=0, tiled=True
    )
    arrived = lax.all_to_all(
        spread[arrive_from], "ep", split_axis=0, concat_axis=0, tiled=True
    ).reshape(half_width, out_width)
    new_grid = grid_of(arrived)
    new_levels = levels_of(arrived, new_grid)
    both_weights = jnp.stack(
        [dequantize(stale_levels, stale_grid), dequantize(new_levels, new_grid)]
    )
    slot_numbers = jnp.arange(experts * capacity, dtype=jnp.int32)
    results = []
    for step_index in range(step_count):
        active = (step_index >= leave_step).astype(jnp.int32)
        weights_now = lax.dynamic_index_in_dim(both_weights, active, 0, keepdims=False)
        target_owner = jnp.where(move_step <= step_index, new_owner, old_owner)
        expert_ids = routes[step_index].reshape(-1)
        token_rows = expert_inputs[step_index].reshape(-1, inner_width)
        matches = expert_ids[:, None] == all_experts[None, :]
        hit_counts = matches.astype(jnp.int32)
        before = jnp.cumsum(hit_counts, axis=0) - hit_counts
        slot_rank = jnp.sum(jnp.where(matches, before, 0), axis=1)
        target_device = jnp.sum(jnp.where(matches, target_owner[None, :], 0), axis=1)
        selector = (target_device * capacity + slot_rank)[:, None] == slot_numbers[None, :]
        outgoing = jnp.dot(
            jnp.transpose(selector).astype(jnp.bfloat16),
            token_rows,
            preferred_element_type=jnp.float32,
        ).astype(jnp.bfloat16)
        outgoing = outgoing.reshape(experts, capacity, 2, half_width)
        arriving = lax.all_to_all(
            lax.all_to_all(outgoing, "ep", split_axis=0, concat_axis=0, tiled=True),
            "sub",
            split_axis=2,
            concat_axis=2,
            tiled=True,
        )
        arriving_rows = arriving.reshape(-1, half_width).astype(jnp.float32)
        running = jnp.dot(arriving_rows, weights_now, precision=lax.Precision.HIGHEST)
        partial_value = running.astype(jnp.bfloat16).reshape(experts, capacity, 2, out_width)
        joined = lax.all_to_all(partial_value, "sub", split_axis=2, concat_axis=2, tiled=True)
        summed = (joined[:, :, 0].astype(jnp.float32) + joined[:, :, 1].astype(jnp.float32)).astype(
            jnp.bfloat16
        )
        returned = lax.all_to_all(summed, "ep", split_axis=0, concat_axis=0, tiled=True)
        weighted = jnp.where(selector, route_weights[step_index].reshape(-1)[:, None], 0.0)
        mixing = jnp.sum(weighted.reshape(token_count, top_count, -1), axis=1)
        combined = jnp.dot(
            mixing,
            returned.reshape(-1, out_width).astype(jnp.float32),
            precision=lax.Precision.HIGHEST,
        )
        results.append(combined.astype(jnp.bfloat16))
    level_output = (new_levels.astype(jnp.float32) * 0.0078125).astype(jnp.bfloat16)[None]
    return (jnp.stack(results), level_output, new_grid[None])


EXTRA_ROWS = 16


def split3(value):
    high = value.astype(jnp.bfloat16)
    rest = value - high.astype(jnp.float32)
    middle = rest.astype(jnp.bfloat16)
    low = (rest - middle.astype(jnp.float32)).astype(jnp.bfloat16)
    return high, middle, low


def raw_levels(weights, step_grid):
    blocks = weights.reshape(step_grid.shape[0], Q_BLOCK, weights.shape[-1])
    nearest = jnp.floor(blocks / step_grid[:, None, :] + 0.5)
    return jnp.clip(nearest, -127.0, 127.0).reshape(weights.shape)


def requantize_kernel(master_ref, piece_ref):
    weights = master_ref[...]
    rows = weights.shape[0]
    step_grid = grid_of(weights)
    levels = raw_levels(weights, step_grid)
    piece_ref[0, 0:rows, :] = (levels * 0.0078125).astype(jnp.bfloat16)
    high, middle, low = split3(step_grid)
    blocks = step_grid.shape[0]
    fill = jnp.zeros((EXTRA_ROWS - 3 * blocks, weights.shape[1]), jnp.float32)
    extra = jnp.concatenate(
        [high.astype(jnp.float32), middle.astype(jnp.float32), low.astype(jnp.float32), fill], axis=0
    )
    piece_ref[0, rows : rows + EXTRA_ROWS, :] = extra.astype(jnp.bfloat16)


def greet(targets):
    barrier = pltpu.get_barrier_semaphore()
    for target in targets:
        pl.semaphore_signal(
            barrier, inc=1, device_id=target, device_id_type=pl.DeviceIdType.MESH
        )
    pl.semaphore_wait(barrier, len(targets))


def dispatch_kernel(
    experts,
    outgoing_ref,
    pieces_ref,
    arriving_ref,
    spread_ref,
    token_send,
    token_recv,
    piece_send,
    piece_recv,
    local_sem,
):
    me = lax.axis_index("ep")
    core = lax.axis_index("sub")
    half = arriving_ref.shape[-1]
    everyone = []
    for offset in range(experts):
        for flip in range(2):
            if offset or flip:
                everyone.append(
                    {"ep": lax.rem(me + offset, experts), "sub": lax.rem(core + flip, 2)}
                )
    greet(everyone)

    def token_copy(offset, flip):
        target = lax.rem(me + offset, experts)
        side = lax.rem(core + flip, 2)
        columns = pl.ds(pl.multiple_of(side * half, 128), half)
        return pltpu.make_async_remote_copy(
            src_ref=outgoing_ref.at[target, :, :, columns],
            dst_ref=arriving_ref.at[:, core, me],
            send_sem=token_send.at[offset, flip],
            recv_sem=token_recv.at[offset, flip],
            device_id={"ep": target, "sub": side},
            device_id_type=pl.DeviceIdType.MESH,
        )

    def piece_copy(offset):
        target = lax.rem(me + offset, experts)
        return pltpu.make_async_remote_copy(
            src_ref=pieces_ref.at[target],
            dst_ref=spread_ref.at[me],
            send_sem=piece_send.at[offset],
            recv_sem=piece_recv.at[offset],
            device_id={"ep": target, "sub": core},
            device_id_type=pl.DeviceIdType.MESH,
        )

    own_tokens = pltpu.make_async_copy(
        outgoing_ref.at[me, :, :, pl.ds(pl.multiple_of(core * half, 128), half)],
        arriving_ref.at[:, core, me],
        local_sem.at[0],
    )
    own_piece = pltpu.make_async_copy(pieces_ref.at[me], spread_ref.at[me], local_sem.at[1])
    token_copies = [
        token_copy(offset, flip) for offset in range(experts) for flip in range(2) if offset or flip
    ]
    piece_copies = [piece_copy(offset) for offset in range(1, experts)]
    for copy in token_copies:
        copy.start()
    own_tokens.start()
    for copy in piece_copies:
        copy.start()
    own_piece.start()
    own_tokens.wait()
    own_piece.wait()
    for copy in token_copies + piece_copies:
        copy.wait()


def serve_kernel(active_ref, rows_ref, master_ref, stale_ref, out_ref):
    weights = master_ref[...]
    stale_grid = stale_ref[...]
    new_grid = grid_of(weights)
    stale_levels = raw_levels(weights, stale_grid)
    new_levels = raw_levels(weights, new_grid)
    for step in range(rows_ref.shape[0]):
        moved = active_ref[step] > 0
        step_grid = jnp.where(moved, new_grid, stale_grid)
        levels = jnp.where(moved, new_levels, stale_levels).astype(jnp.bfloat16)
        total = None
        for block in range(step_grid.shape[0]):
            here = slice(block * Q_BLOCK, (block + 1) * Q_BLOCK)
            product = jnp.dot(
                rows_ref[step, :, here], levels[here], preferred_element_type=jnp.float32
            )
            product = product * step_grid[block : block + 1, :]
            total = product if total is None else total + product
        out_ref[step] = total.astype(jnp.bfloat16)


def combine_kernel(
    experts,
    partial_ref,
    chosen_ref,
    mixed_ref,
    arrived_ref,
    other_ref,
    send_one,
    recv_one,
    send_two,
    recv_two,
    send_three,
    recv_three,
    other_sems,
    one_sems,
    two_sems,
    three_sems,
    piece_send,
    piece_recv,
    local_sem,
):
    me = lax.axis_index("ep")
    core = lax.axis_index("sub")
    planes = experts // 4
    x = lax.rem(me, 2)
    y = lax.rem(me // 2, 2)
    z = me // 4
    half = partial_ref.shape[-1] // 2
    piece_columns = chosen_ref.shape[-1]
    MESH = pl.DeviceIdType.MESH
    peers = [{"ep": lax.rem(me + offset, experts), "sub": core} for offset in range(1, experts)]
    partner = {"ep": me, "sub": 1 - core}
    greet(peers + [partner])
    sides = [slice(0, half), slice(half, 2 * half)]
    across_x = {"ep": z * 4 + y * 2 + (1 - x), "sub": core}
    across_y = {"ep": z * 4 + (1 - y) * 2 + x, "sub": core}

    other_copies = []
    for side in range(2):
        copy = pltpu.make_async_remote_copy(
            src_ref=partial_ref.at[:, 1 - core, :, :, sides[side]],
            dst_ref=other_ref.at[:, :, :, sides[side]],
            send_sem=other_sems.at[0, side],
            recv_sem=other_sems.at[1, side],
            device_id=partner,
            device_id_type=MESH,
        )
        copy.start()
        other_copies.append(copy)

    columns = pl.ds(pl.multiple_of(me * piece_columns, 128), piece_columns)
    piece_copies = []
    for offset in range(1, experts):
        target = lax.rem(me + offset, experts)
        copy = pltpu.make_async_remote_copy(
            src_ref=chosen_ref.at[target],
            dst_ref=arrived_ref.at[:, columns],
            send_sem=piece_send.at[offset],
            recv_sem=piece_recv.at[offset],
            device_id={"ep": target, "sub": core},
            device_id_type=MESH,
        )
        piece_copies.append(copy)
    own_piece = pltpu.make_async_copy(chosen_ref.at[me], arrived_ref.at[:, columns], local_sem.at[0])

    def pair(target, side):
        here = sides[side]
        return partial_ref[:, core, target, :, here].astype(jnp.float32) + other_ref[
            :, target, :, here
        ].astype(jnp.float32)

    def send(source, landing, sems, side, device):
        copy = pltpu.make_async_remote_copy(
            src_ref=source.at[side],
            dst_ref=landing.at[side],
            send_sem=sems.at[0, side],
            recv_sem=sems.at[1, side],
            device_id=device,
            device_id_type=MESH,
        )
        copy.start()
        return copy

    one_copies = []
    for side in range(2):
        other_copies[side].wait()

        def first(number, carry, side=side):
            plane, place = number // 2, lax.rem(number, 2)
            if side == 0:
                target = plane * 4 + place * 2 + (1 - x)
            else:
                target = plane * 4 + (1 - y) * 2 + place
            send_one[side, number] = pair(target, side).astype(jnp.bfloat16)
            return carry

        lax.fori_loop(0, 2 * planes, first, 0)
        one_copies.append(
            send(send_one, recv_one, one_sems, side, across_x if side == 0 else across_y)
        )

    for copy in piece_copies:
        copy.start()
    own_piece.start()

    two_copies = []
    for side in range(2):
        one_copies[side].wait()

        def second(plane, carry, side=side):
            if side == 0:
                target, number = plane * 4 + (1 - y) * 2 + x, plane * 2 + (1 - y)
            else:
                target, number = plane * 4 + y * 2 + (1 - x), plane * 2 + (1 - x)
            value = pair(target, side) + recv_one[side, number].astype(jnp.float32)
            send_two[side, plane] = value.astype(jnp.bfloat16)
            return carry

        lax.fori_loop(0, planes, second, 0)
        two_copies.append(
            send(send_two, recv_two, two_sems, side, across_y if side == 0 else across_x)
        )

    def third_value(plane, side):
        target = plane * 4 + y * 2 + x
        number = plane * 2 + (y if side == 0 else x)
        return (
            pair(target, side)
            + recv_one[side, number].astype(jnp.float32)
            + recv_two[side, plane].astype(jnp.float32)
        )

    for side in range(2):
        two_copies[side].wait()
    three_copies = []
    for offset in range(1, planes):
        plane = lax.rem(z + offset, planes)
        for side in range(2):
            send_three[offset - 1, :, :, sides[side]] = third_value(plane, side).astype(
                jnp.bfloat16
            )
        copy = pltpu.make_async_remote_copy(
            src_ref=send_three.at[offset - 1],
            dst_ref=recv_three.at[offset - 1],
            send_sem=three_sems.at[0, offset],
            recv_sem=three_sems.at[1, offset],
            device_id={"ep": plane * 4 + y * 2 + x, "sub": core},
            device_id_type=MESH,
        )
        copy.start()
        three_copies.append(copy)
    for copy in three_copies:
        copy.wait()
    for side in range(2):
        total = third_value(z, side)
        for offset in range(1, planes):
            total = total + recv_three[offset - 1, :, :, sides[side]].astype(jnp.float32)
        mixed_ref[:, :, sides[side]] = total.astype(jnp.bfloat16)
    own_piece.wait()
    for copy in piece_copies:
        copy.wait()


def local_small(expert_inputs, routes, route_weights, master, old_steps, move_list):
    experts = lax.axis_size("ep")
    my_index = lax.axis_index("ep")
    steps, tokens, top, inner = expert_inputs.shape
    half, width = master.shape[1:]
    piece_columns = width // experts
    piece_rows = half + EXTRA_ROWS
    any_space = pl.BlockSpec(memory_space=pl.ANY)
    vmem = pl.BlockSpec(memory_space=pltpu.VMEM)
    expert_column, old_column = move_list[:, 0], move_list[:, 1]
    new_column, step_column = move_list[:, 2], move_list[:, 3]
    all_experts = jnp.arange(experts, dtype=jnp.int32)
    old_owner = lookup(expert_column, old_column, all_experts)
    arrive_from = lookup(new_column, old_column, all_experts)
    leave_step = lookup(old_column, step_column, jnp.reshape(my_index, (1,)))[0]
    active = (jnp.arange(steps, dtype=jnp.int32) >= leave_step).astype(jnp.int32)

    pieces = pl.pallas_call(
        requantize_kernel,
        out_shape=jax.ShapeDtypeStruct((experts, piece_rows, piece_columns), jnp.bfloat16),
        grid=(experts,),
        in_specs=[pl.BlockSpec((half, piece_columns), lambda i: (0, i))],
        out_specs=pl.BlockSpec((1, piece_rows, piece_columns), lambda i: (i, 0, 0)),
    )(master[0])

    pairs = steps * tokens * top
    ids = routes.reshape(pairs)
    target = jnp.sum(
        jnp.where(ids[:, None] == all_experts[None, :], old_owner[None, :], 0), axis=1
    )
    pair_numbers = jnp.arange(pairs, dtype=jnp.int32)
    slot_numbers = jnp.arange(experts * steps * tokens, dtype=jnp.int32)
    slot = target * (steps * tokens) + pair_numbers // top
    selector = (slot[None, :] == slot_numbers[:, None]).astype(jnp.bfloat16)
    rows = expert_inputs.reshape(pairs, inner).astype(jnp.float32)
    rows = (rows * route_weights.reshape(pairs)[:, None]).astype(jnp.bfloat16)
    outgoing = jnp.dot(selector, rows, preferred_element_type=jnp.float32).astype(jnp.bfloat16)
    outgoing = outgoing.reshape(experts, steps, tokens, inner)

    arriving, spread = pl.pallas_call(
        functools.partial(dispatch_kernel, experts),
        out_shape=(
            jax.ShapeDtypeStruct((steps, 2, experts, tokens, half), jnp.bfloat16),
            jax.ShapeDtypeStruct((experts, piece_rows, piece_columns), jnp.bfloat16),
        ),
        in_specs=[any_space, any_space],
        out_specs=(any_space, any_space),
        scratch_shapes=[
            pltpu.SemaphoreType.DMA((experts, 2)),
            pltpu.SemaphoreType.DMA((experts, 2)),
            pltpu.SemaphoreType.DMA((experts,)),
            pltpu.SemaphoreType.DMA((experts,)),
            pltpu.SemaphoreType.DMA((2,)),
        ],
        compiler_params=pltpu.CompilerParams(collective_id=0, has_side_effects=True),
    )(outgoing, pieces)

    row_count = 2 * experts * tokens
    tile = 256
    blocks = half // Q_BLOCK
    partial = pl.pallas_call(
        serve_kernel,
        out_shape=jax.ShapeDtypeStruct((steps, row_count, width), jnp.bfloat16),
        grid=(width // tile,),
        in_specs=[
            pl.BlockSpec(memory_space=pltpu.SMEM),
            pl.BlockSpec((steps, row_count, half), lambda i: (0, 0, 0)),
            pl.BlockSpec((half, tile), lambda i: (0, i)),
            pl.BlockSpec((blocks, tile), lambda i: (0, i)),
        ],
        out_specs=pl.BlockSpec((steps, row_count, tile), lambda i: (0, 0, i)),
        compiler_params=pltpu.CompilerParams(vmem_limit_bytes=40 * 1024 * 1024),
    )(active, arriving.reshape(steps, row_count, half), master[0], old_steps[0])
    partial = partial.reshape(steps, 2, experts, tokens, width)
    chosen = spread[arrive_from]

    planes = experts // 4
    mixed, arrived = pl.pallas_call(
        functools.partial(combine_kernel, experts),
        out_shape=(
            jax.ShapeDtypeStruct((steps, tokens, width), jnp.bfloat16),
            jax.ShapeDtypeStruct((piece_rows, width), jnp.bfloat16),
        ),
        in_specs=[vmem, any_space],
        out_specs=(vmem, any_space),
        scratch_shapes=[
            pltpu.VMEM((steps, experts, tokens, width), jnp.bfloat16),
            pltpu.VMEM((2, 2 * planes, steps, tokens, width // 2), jnp.bfloat16),
            pltpu.VMEM((2, 2 * planes, steps, tokens, width // 2), jnp.bfloat16),
            pltpu.VMEM((2, planes, steps, tokens, width // 2), jnp.bfloat16),
            pltpu.VMEM((2, planes, steps, tokens, width // 2), jnp.bfloat16),
            pltpu.VMEM((planes - 1, steps, tokens, width), jnp.bfloat16),
            pltpu.VMEM((planes - 1, steps, tokens, width), jnp.bfloat16),
            pltpu.SemaphoreType.DMA((2, 2)),
            pltpu.SemaphoreType.DMA((2, 2)),
            pltpu.SemaphoreType.DMA((2, 2)),
            pltpu.SemaphoreType.DMA((2, planes)),
            pltpu.SemaphoreType.DMA((experts,)),
            pltpu.SemaphoreType.DMA((experts,)),
            pltpu.SemaphoreType.DMA((1,)),
        ],
        compiler_params=pltpu.CompilerParams(
            collective_id=1, has_side_effects=True, vmem_limit_bytes=48 * 1024 * 1024
        ),
    )(partial, chosen)
    parts = arrived[half : half + 3 * blocks].astype(jnp.float32).reshape(3, blocks, width)
    new_steps = (parts[0] + parts[1]) + parts[2]
    return mixed, arrived[:half][None], new_steps[None]


def body_for(mesh):
    def body(expert_inputs, routes, route_weights, master, old_steps, move_list):
        experts, cores = mesh.shape["ep"], mesh.shape["sub"]
        tokens, top = routes.shape[1:]
        half, width = master.shape[1:]
        fits = (
            experts % 4 == 0
            and experts <= 16
            and cores == 2
            and tokens % 16 == 0
            and width % (experts * 128) == 0
            and half % Q_BLOCK == 0
            and 3 * (half // Q_BLOCK) <= EXTRA_ROWS
        )
        chosen = local_small if fits else local
        return chosen(expert_inputs, routes, route_weights, master, old_steps, move_list)

    return body


def solution(mesh):
    placed = (
        P(None, ("groups", "ep", "sub"), None, None),
        P(None, ("groups", "ep", "sub"), None),
        P(None, ("groups", "ep", "sub"), None),
        P("ep", "sub", None),
        P("ep", "sub", None),
        P(),
    )
    return jax.shard_map(
        body_for(mesh),
        mesh=mesh,
        in_specs=placed,
        out_specs=(
            P(None, ("groups", "ep", "sub"), None),
            P(("groups", "ep"), "sub", None),
            P(("groups", "ep"), "sub", None),
        ),
        check_vma=False,
    )
```

```python
import functools

import jax
import jax.numpy as jnp
from jax import lax
from jax.experimental import pallas as pl
from jax.experimental.pallas import tpu as pltpu
from jax.sharding import PartitionSpec as P

Q_BLOCK = 128


EPSILON = 1e-06


def grid_of(weights):
    blocks = weights.reshape(-1, Q_BLOCK, weights.shape[-1])
    return (jnp.max(jnp.abs(blocks), axis=1) + EPSILON) / 127.0


def levels_of(weights, step_grid):
    blocks = weights.reshape(step_grid.shape[0], Q_BLOCK, weights.shape[-1])
    nearest = jnp.floor(blocks / step_grid[:, None, :] + 0.5)
    return jnp.clip(nearest, -127.0, 127.0).reshape(weights.shape).astype(jnp.bfloat16)


def dequantize(levels, step_grid):
    blocks = levels.reshape(step_grid.shape[0], Q_BLOCK, levels.shape[-1]).astype(jnp.float32)
    return (blocks * step_grid[:, None, :]).reshape(levels.shape)


def lookup(key_column, value_column, queries):
    matches = key_column[None, :] == queries[:, None]
    return jnp.sum(jnp.where(matches, value_column[None, :], 0), axis=1)


def local(expert_inputs, routes, route_weights, master, old_steps, move_list):
    experts = lax.axis_size("ep")
    my_index = lax.axis_index("ep")
    step_count, token_count, top_count, inner_width = expert_inputs.shape
    half_width = master.shape[1]
    out_width = master.shape[2]
    capacity = min(token_count, max(2, 2 * token_count * top_count // experts))
    all_experts = jnp.arange(experts, dtype=jnp.int32)
    expert_column = move_list[:, 0]
    old_column = move_list[:, 1]
    new_column = move_list[:, 2]
    step_column = move_list[:, 3]
    old_owner = lookup(expert_column, old_column, all_experts)
    new_owner = lookup(expert_column, new_column, all_experts)
    move_step = lookup(expert_column, step_column, all_experts)
    arrive_from = lookup(new_column, old_column, all_experts)
    leave_step = lookup(old_column, step_column, jnp.reshape(my_index, (1,)))[0]
    own_master = master[0]
    stale_grid = old_steps[0]
    stale_levels = levels_of(own_master, stale_grid)
    spread = lax.all_to_all(
        own_master.reshape(experts, -1), "ep", split_axis=0, concat_axis=0, tiled=True
    )
    arrived = lax.all_to_all(
        spread[arrive_from], "ep", split_axis=0, concat_axis=0, tiled=True
    ).reshape(half_width, out_width)
    new_grid = grid_of(arrived)
    new_levels = levels_of(arrived, new_grid)
    both_weights = jnp.stack(
        [dequantize(stale_levels, stale_grid), dequantize(new_levels, new_grid)]
    )
    slot_numbers = jnp.arange(experts * capacity, dtype=jnp.int32)
    results = []
    for step_index in range(step_count):
        active = (step_index >= leave_step).astype(jnp.int32)
        weights_now = lax.dynamic_index_in_dim(both_weights, active, 0, keepdims=False)
        target_owner = jnp.where(move_step <= step_index, new_owner, old_owner)
        expert_ids = routes[step_index].reshape(-1)
        token_rows = expert_inputs[step_index].reshape(-1, inner_width)
        matches = expert_ids[:, None] == all_experts[None, :]
        hit_counts = matches.astype(jnp.int32)
        before = jnp.cumsum(hit_counts, axis=0) - hit_counts
        slot_rank = jnp.sum(jnp.where(matches, before, 0), axis=1)
        target_device = jnp.sum(jnp.where(matches, target_owner[None, :], 0), axis=1)
        selector = (target_device * capacity + slot_rank)[:, None] == slot_numbers[None, :]
        outgoing = jnp.dot(
            jnp.transpose(selector).astype(jnp.bfloat16),
            token_rows,
            preferred_element_type=jnp.float32,
        ).astype(jnp.bfloat16)
        outgoing = outgoing.reshape(experts, capacity, 2, half_width)
        arriving = lax.all_to_all(
            lax.all_to_all(outgoing, "ep", split_axis=0, concat_axis=0, tiled=True),
            "sub",
            split_axis=2,
            concat_axis=2,
            tiled=True,
        )
        arriving_rows = arriving.reshape(-1, half_width).astype(jnp.float32)
        running = jnp.dot(arriving_rows, weights_now, precision=lax.Precision.HIGHEST)
        partial_value = running.astype(jnp.bfloat16).reshape(experts, capacity, 2, out_width)
        joined = lax.all_to_all(partial_value, "sub", split_axis=2, concat_axis=2, tiled=True)
        summed = (joined[:, :, 0].astype(jnp.float32) + joined[:, :, 1].astype(jnp.float32)).astype(
            jnp.bfloat16
        )
        returned = lax.all_to_all(summed, "ep", split_axis=0, concat_axis=0, tiled=True)
        weighted = jnp.where(selector, route_weights[step_index].reshape(-1)[:, None], 0.0)
        mixing = jnp.sum(weighted.reshape(token_count, top_count, -1), axis=1)
        combined = jnp.dot(
            mixing,
            returned.reshape(-1, out_width).astype(jnp.float32),
            precision=lax.Precision.HIGHEST,
        )
        results.append(combined.astype(jnp.bfloat16))
    level_output = (new_levels.astype(jnp.float32) * 0.0078125).astype(jnp.bfloat16)[None]
    return (jnp.stack(results), level_output, new_grid[None])


EXTRA_ROWS = 16


def split3(value):
    high = value.astype(jnp.bfloat16)
    rest = value - high.astype(jnp.float32)
    middle = rest.astype(jnp.bfloat16)
    low = (rest - middle.astype(jnp.float32)).astype(jnp.bfloat16)
    return high, middle, low


def raw_levels(weights, step_grid):
    blocks = weights.reshape(step_grid.shape[0], Q_BLOCK, weights.shape[-1])
    nearest = jnp.floor(blocks / step_grid[:, None, :] + 0.5)
    return jnp.clip(nearest, -127.0, 127.0).reshape(weights.shape)


def greet(targets):
    barrier = pltpu.get_barrier_semaphore()
    for target in targets:
        pl.semaphore_signal(
            barrier, inc=1, device_id=target, device_id_type=pl.DeviceIdType.MESH
        )
    pl.semaphore_wait(barrier, len(targets))


def whole_kernel(
    experts,
    arrive_ref,
    active_ref,
    outgoing_ref,
    master_ref,
    stale_ref,
    mixed_ref,
    arrived_ref,
    arriving_ref,
    levels_ref,
    grids_ref,
    pieces_ref,
    spread_ref,
    chosen_ref,
    partial_ref,
    other_ref,
    send_one,
    recv_one,
    send_two,
    recv_two,
    send_three,
    recv_three,
    token_send,
    token_recv,
    spread_sems,
    move_sems,
    other_sems,
    one_sems,
    two_sems,
    three_sems,
    local_sem,
):
    me = lax.axis_index("ep")
    core = lax.axis_index("sub")
    steps, _, _, tokens, rows = arriving_ref.shape
    blocks = rows // Q_BLOCK
    width = partial_ref.shape[-1]
    piece_columns = width // experts
    planes = experts // 4
    x = lax.rem(me, 2)
    y = lax.rem(me // 2, 2)
    z = me // 4
    half = width // 2
    MESH = pl.DeviceIdType.MESH
    everyone = []
    for offset in range(experts):
        for flip in range(2):
            if offset or flip:
                everyone.append(
                    {"ep": lax.rem(me + offset, experts), "sub": lax.rem(core + flip, 2)}
                )
    greet(everyone)

    def token_copy(offset, flip):
        target = lax.rem(me + offset, experts)
        side = lax.rem(core + flip, 2)
        columns = pl.ds(pl.multiple_of(side * rows, 128), rows)
        return pltpu.make_async_remote_copy(
            src_ref=outgoing_ref.at[target, :, :, columns],
            dst_ref=arriving_ref.at[:, core, me],
            send_sem=token_send.at[offset, flip],
            recv_sem=token_recv.at[offset, flip],
            device_id={"ep": target, "sub": side},
            device_id_type=MESH,
        )

    token_copies = [
        token_copy(offset, flip) for offset in range(experts) for flip in range(2) if offset or flip
    ]
    for copy in token_copies:
        copy.start()
    own_tokens = pltpu.make_async_copy(
        outgoing_ref.at[me, :, :, pl.ds(pl.multiple_of(core * rows, 128), rows)],
        arriving_ref.at[:, core, me],
        local_sem.at[0],
    )
    own_tokens.start()

    def requantize(piece, carry):
        columns = pl.ds(pl.multiple_of(piece * piece_columns, 128), piece_columns)
        weights = master_ref[:, columns]
        stale_grid = stale_ref[:, columns]
        new_grid = grid_of(weights)
        new_levels = raw_levels(weights, new_grid)
        stale_levels = raw_levels(weights, stale_grid)
        pieces_ref[piece, 0:rows, :] = (new_levels * 0.0078125).astype(jnp.bfloat16)
        high, middle, low = split3(new_grid)
        fill = jnp.zeros((EXTRA_ROWS - 3 * blocks, piece_columns), jnp.float32)
        parts = [part.astype(jnp.float32) for part in (high, middle, low)]
        extra = jnp.concatenate(parts + [fill], axis=0)
        pieces_ref[piece, rows : rows + EXTRA_ROWS, :] = extra.astype(jnp.bfloat16)
        for step in range(steps):
            moved = active_ref[step : step + 1, :] > 0
            grids_ref[step, 0:blocks, columns] = jnp.where(moved, new_grid, stale_grid)
            levels_ref[step, :, columns] = jnp.where(moved, new_levels, stale_levels).astype(
                jnp.bfloat16
            )
        return carry

    lax.fori_loop(0, experts, requantize, 0)

    spread_copies = []
    for offset in range(1, experts):
        target = lax.rem(me + offset, experts)
        copy = pltpu.make_async_remote_copy(
            src_ref=pieces_ref.at[target],
            dst_ref=spread_ref.at[me],
            send_sem=spread_sems.at[0, offset],
            recv_sem=spread_sems.at[1, offset],
            device_id={"ep": target, "sub": core},
            device_id_type=MESH,
        )
        copy.start()
        spread_copies.append(copy)
    own_spread = pltpu.make_async_copy(pieces_ref.at[me], spread_ref.at[me], local_sem.at[1])
    own_spread.start()

    own_tokens.wait()
    for copy in token_copies:
        copy.wait_recv()

    tile = min(256, width)

    def serve(number, carry):
        columns = pl.ds(pl.multiple_of(number * tile, 128), tile)
        for step in range(steps):
            token_rows = arriving_ref[step].reshape(2 * experts * tokens, rows)
            total = None
            for block in range(blocks):
                here = slice(block * Q_BLOCK, (block + 1) * Q_BLOCK)
                product = jnp.dot(
                    token_rows[:, here],
                    levels_ref[step, here, columns],
                    preferred_element_type=jnp.float32,
                )
                product = product * grids_ref[step, block : block + 1, columns]
                total = product if total is None else total + product
            partial_ref[step, :, :, :, columns] = total.reshape(
                2, experts, tokens, tile
            ).astype(jnp.bfloat16)
        return carry

    sides = [slice(0, half), slice(half, 2 * half)]
    across_x = {"ep": z * 4 + y * 2 + (1 - x), "sub": core}
    across_y = {"ep": z * 4 + (1 - y) * 2 + x, "sub": core}
    other_copies = []
    tiles = half // tile
    for side in range(2):
        lax.fori_loop(side * tiles, (side + 1) * tiles, serve, 0)
        copy = pltpu.make_async_remote_copy(
            src_ref=partial_ref.at[:, 1 - core, :, :, sides[side]],
            dst_ref=other_ref.at[:, :, :, sides[side]],
            send_sem=other_sems.at[0, side],
            recv_sem=other_sems.at[1, side],
            device_id={"ep": me, "sub": 1 - core},
            device_id_type=MESH,
        )
        copy.start()
        other_copies.append(copy)

    def pair(target, side):
        here = sides[side]
        return partial_ref[:, core, target, :, here].astype(jnp.float32) + other_ref[
            :, target, :, here
        ].astype(jnp.float32)

    def send(source, landing, sems, side, device):
        copy = pltpu.make_async_remote_copy(
            src_ref=source.at[side],
            dst_ref=landing.at[side],
            send_sem=sems.at[0, side],
            recv_sem=sems.at[1, side],
            device_id=device,
            device_id_type=MESH,
        )
        copy.start()
        return copy

    one_copies = []
    for side in range(2):
        other_copies[side].wait()

        def first(number, carry, side=side):
            plane, place = number // 2, lax.rem(number, 2)
            if side == 0:
                target = plane * 4 + place * 2 + (1 - x)
            else:
                target = plane * 4 + (1 - y) * 2 + place
            send_one[side, number] = pair(target, side).astype(jnp.bfloat16)
            return carry

        lax.fori_loop(0, 2 * planes, first, 0)
        one_copies.append(
            send(send_one, recv_one, one_sems, side, across_x if side == 0 else across_y)
        )

    two_copies = []
    for side in range(2):
        one_copies[side].wait()

        def second(plane, carry, side=side):
            if side == 0:
                target, number = plane * 4 + (1 - y) * 2 + x, plane * 2 + (1 - y)
            else:
                target, number = plane * 4 + y * 2 + (1 - x), plane * 2 + (1 - x)
            value = pair(target, side) + recv_one[side, number].astype(jnp.float32)
            send_two[side, plane] = value.astype(jnp.bfloat16)
            return carry

        lax.fori_loop(0, planes, second, 0)
        two_copies.append(
            send(send_two, recv_two, two_sems, side, across_y if side == 0 else across_x)
        )

    def third_value(plane, side):
        target = plane * 4 + y * 2 + x
        number = plane * 2 + (y if side == 0 else x)
        return (
            pair(target, side)
            + recv_one[side, number].astype(jnp.float32)
            + recv_two[side, plane].astype(jnp.float32)
        )

    own_spread.wait()
    for copy in spread_copies:
        copy.wait()

    def choose(number, carry):
        chosen_ref[number] = spread_ref[arrive_ref[number]]
        return carry

    lax.fori_loop(0, experts, choose, 0)
    columns = pl.ds(pl.multiple_of(me * piece_columns, 128), piece_columns)
    piece_copies = []
    for offset in range(1, experts):
        target = lax.rem(me + offset, experts)
        copy = pltpu.make_async_remote_copy(
            src_ref=chosen_ref.at[target],
            dst_ref=arrived_ref.at[:, columns],
            send_sem=move_sems.at[0, offset],
            recv_sem=move_sems.at[1, offset],
            device_id={"ep": target, "sub": core},
            device_id_type=MESH,
        )
        copy.start()
        piece_copies.append(copy)
    own_piece = pltpu.make_async_copy(chosen_ref.at[me], arrived_ref.at[:, columns], local_sem.at[2])
    own_piece.start()

    for side in range(2):
        two_copies[side].wait()
    three_copies = []
    for offset in range(1, planes):
        plane = lax.rem(z + offset, planes)
        for side in range(2):
            send_three[offset - 1, :, :, sides[side]] = third_value(plane, side).astype(
                jnp.bfloat16
            )
        copy = pltpu.make_async_remote_copy(
            src_ref=send_three.at[offset - 1],
            dst_ref=recv_three.at[offset - 1],
            send_sem=three_sems.at[0, offset],
            recv_sem=three_sems.at[1, offset],
            device_id={"ep": plane * 4 + y * 2 + x, "sub": core},
            device_id_type=MESH,
        )
        copy.start()
        three_copies.append(copy)
    for copy in three_copies:
        copy.wait()
    for side in range(2):
        total = third_value(z, side)
        for offset in range(1, planes):
            total = total + recv_three[offset - 1, :, :, sides[side]].astype(jnp.float32)
        mixed_ref[:, :, sides[side]] = total.astype(jnp.bfloat16)
    own_piece.wait()
    for copy in piece_copies:
        copy.wait()
    for copy in token_copies:
        copy.wait_send()


def local_small(expert_inputs, routes, route_weights, master, old_steps, move_list):
    experts = lax.axis_size("ep")
    my_index = lax.axis_index("ep")
    steps, tokens, top, inner = expert_inputs.shape
    half, width = master.shape[1:]
    piece_columns = width // experts
    piece_rows = half + EXTRA_ROWS
    any_space = pl.BlockSpec(memory_space=pl.ANY)
    vmem = pl.BlockSpec(memory_space=pltpu.VMEM)
    expert_column, old_column = move_list[:, 0], move_list[:, 1]
    new_column, step_column = move_list[:, 2], move_list[:, 3]
    all_experts = jnp.arange(experts, dtype=jnp.int32)
    old_owner = lookup(expert_column, old_column, all_experts)
    arrive_from = lookup(new_column, old_column, all_experts)
    leave_step = lookup(old_column, step_column, jnp.reshape(my_index, (1,)))[0]
    active = (jnp.arange(steps, dtype=jnp.int32) >= leave_step).astype(jnp.int32)
    active = jnp.broadcast_to(active[:, None], (steps, piece_columns))

    pairs = steps * tokens * top
    ids = routes.reshape(pairs)
    target = jnp.sum(
        jnp.where(ids[:, None] == all_experts[None, :], old_owner[None, :], 0), axis=1
    )
    pair_numbers = jnp.arange(pairs, dtype=jnp.int32)
    slot_numbers = jnp.arange(experts * steps * tokens, dtype=jnp.int32)
    slot = target * (steps * tokens) + pair_numbers // top
    selector = (slot[None, :] == slot_numbers[:, None]).astype(jnp.bfloat16)
    rows = expert_inputs.reshape(pairs, inner).astype(jnp.float32)
    rows = (rows * route_weights.reshape(pairs)[:, None]).astype(jnp.bfloat16)
    outgoing = jnp.dot(selector, rows, preferred_element_type=jnp.float32).astype(jnp.bfloat16)
    outgoing = outgoing.reshape(experts, steps, tokens, inner)

    blocks = half // Q_BLOCK
    planes = experts // 4
    bf16 = jnp.bfloat16
    mixed, arrived = pl.pallas_call(
        functools.partial(whole_kernel, experts),
        out_shape=(
            jax.ShapeDtypeStruct((steps, tokens, width), bf16),
            jax.ShapeDtypeStruct((piece_rows, width), bf16),
        ),
        in_specs=[pl.BlockSpec(memory_space=pltpu.SMEM), vmem, any_space, vmem, vmem],
        out_specs=(vmem, any_space),
        scratch_shapes=[
            pltpu.VMEM((steps, 2, experts, tokens, half), bf16),
            pltpu.VMEM((steps, half, width), bf16),
            pltpu.VMEM((steps, max(8, blocks), width), jnp.float32),
            pltpu.VMEM((experts, piece_rows, piece_columns), bf16),
            pltpu.VMEM((experts, piece_rows, piece_columns), bf16),
            pltpu.VMEM((experts, piece_rows, piece_columns), bf16),
            pltpu.VMEM((steps, 2, experts, tokens, width), bf16),
            pltpu.VMEM((steps, experts, tokens, width), bf16),
            pltpu.VMEM((2, 2 * planes, steps, tokens, width // 2), bf16),
            pltpu.VMEM((2, 2 * planes, steps, tokens, width // 2), bf16),
            pltpu.VMEM((2, planes, steps, tokens, width // 2), bf16),
            pltpu.VMEM((2, planes, steps, tokens, width // 2), bf16),
            pltpu.VMEM((planes - 1, steps, tokens, width), bf16),
            pltpu.VMEM((planes - 1, steps, tokens, width), bf16),
            pltpu.SemaphoreType.DMA((experts, 2)),
            pltpu.SemaphoreType.DMA((experts, 2)),
            pltpu.SemaphoreType.DMA((2, experts)),
            pltpu.SemaphoreType.DMA((2, experts)),
            pltpu.SemaphoreType.DMA((2, 2)),
            pltpu.SemaphoreType.DMA((2, 2)),
            pltpu.SemaphoreType.DMA((2, 2)),
            pltpu.SemaphoreType.DMA((2, planes)),
            pltpu.SemaphoreType.DMA((3,)),
        ],
        compiler_params=pltpu.CompilerParams(
            collective_id=0, has_side_effects=True, vmem_limit_bytes=52 * 1024 * 1024
        ),
    )(arrive_from, active, outgoing, master[0], old_steps[0])
    parts = arrived[half : half + 3 * blocks].astype(jnp.float32).reshape(3, blocks, width)
    new_steps = (parts[0] + parts[1]) + parts[2]
    return mixed, arrived[:half][None], new_steps[None]


def body_for(mesh):
    def body(expert_inputs, routes, route_weights, master, old_steps, move_list):
        experts, cores = mesh.shape["ep"], mesh.shape["sub"]
        tokens, top = routes.shape[1:]
        half, width = master.shape[1:]
        fits = (
            experts % 4 == 0
            and experts <= 16
            and cores == 2
            and tokens % 16 == 0
            and width % (experts * 128) == 0
            and half % Q_BLOCK == 0
            and 3 * (half // Q_BLOCK) <= EXTRA_ROWS
        )
        chosen = local_small if fits else local
        return chosen(expert_inputs, routes, route_weights, master, old_steps, move_list)

    return body


def solution(mesh):
    placed = (
        P(None, ("groups", "ep", "sub"), None, None),
        P(None, ("groups", "ep", "sub"), None),
        P(None, ("groups", "ep", "sub"), None),
        P("ep", "sub", None),
        P("ep", "sub", None),
        P(),
    )
    return jax.shard_map(
        body_for(mesh),
        mesh=mesh,
        in_specs=placed,
        out_specs=(
            P(None, ("groups", "ep", "sub"), None),
            P(("groups", "ep"), "sub", None),
            P(("groups", "ep"), "sub", None),
        ),
        check_vma=False,
    )
```

```python
import functools

import jax
import jax.numpy as jnp
from jax import lax
from jax.experimental import pallas as pl
from jax.experimental.pallas import tpu as pltpu
from jax.sharding import PartitionSpec as P

Q_BLOCK = 128


EPSILON = 1e-06


def grid_of(weights):
    blocks = weights.reshape(-1, Q_BLOCK, weights.shape[-1])
    return (jnp.max(jnp.abs(blocks), axis=1) + EPSILON) / 127.0


def levels_of(weights, step_grid):
    blocks = weights.reshape(step_grid.shape[0], Q_BLOCK, weights.shape[-1])
    nearest = jnp.floor(blocks / step_grid[:, None, :] + 0.5)
    return jnp.clip(nearest, -127.0, 127.0).reshape(weights.shape).astype(jnp.bfloat16)


def dequantize(levels, step_grid):
    blocks = levels.reshape(step_grid.shape[0], Q_BLOCK, levels.shape[-1]).astype(jnp.float32)
    return (blocks * step_grid[:, None, :]).reshape(levels.shape)


def lookup(key_column, value_column, queries):
    matches = key_column[None, :] == queries[:, None]
    return jnp.sum(jnp.where(matches, value_column[None, :], 0), axis=1)


def local(expert_inputs, routes, route_weights, master, old_steps, move_list):
    experts = lax.axis_size("ep")
    my_index = lax.axis_index("ep")
    step_count, token_count, top_count, inner_width = expert_inputs.shape
    half_width = master.shape[1]
    out_width = master.shape[2]
    capacity = min(token_count, max(2, 2 * token_count * top_count // experts))
    all_experts = jnp.arange(experts, dtype=jnp.int32)
    expert_column = move_list[:, 0]
    old_column = move_list[:, 1]
    new_column = move_list[:, 2]
    step_column = move_list[:, 3]
    old_owner = lookup(expert_column, old_column, all_experts)
    new_owner = lookup(expert_column, new_column, all_experts)
    move_step = lookup(expert_column, step_column, all_experts)
    arrive_from = lookup(new_column, old_column, all_experts)
    leave_step = lookup(old_column, step_column, jnp.reshape(my_index, (1,)))[0]
    own_master = master[0]
    stale_grid = old_steps[0]
    stale_levels = levels_of(own_master, stale_grid)
    spread = lax.all_to_all(
        own_master.reshape(experts, -1), "ep", split_axis=0, concat_axis=0, tiled=True
    )
    arrived = lax.all_to_all(
        spread[arrive_from], "ep", split_axis=0, concat_axis=0, tiled=True
    ).reshape(half_width, out_width)
    new_grid = grid_of(arrived)
    new_levels = levels_of(arrived, new_grid)
    both_weights = jnp.stack(
        [dequantize(stale_levels, stale_grid), dequantize(new_levels, new_grid)]
    )
    slot_numbers = jnp.arange(experts * capacity, dtype=jnp.int32)
    results = []
    for step_index in range(step_count):
        active = (step_index >= leave_step).astype(jnp.int32)
        weights_now = lax.dynamic_index_in_dim(both_weights, active, 0, keepdims=False)
        target_owner = jnp.where(move_step <= step_index, new_owner, old_owner)
        expert_ids = routes[step_index].reshape(-1)
        token_rows = expert_inputs[step_index].reshape(-1, inner_width)
        matches = expert_ids[:, None] == all_experts[None, :]
        hit_counts = matches.astype(jnp.int32)
        before = jnp.cumsum(hit_counts, axis=0) - hit_counts
        slot_rank = jnp.sum(jnp.where(matches, before, 0), axis=1)
        target_device = jnp.sum(jnp.where(matches, target_owner[None, :], 0), axis=1)
        selector = (target_device * capacity + slot_rank)[:, None] == slot_numbers[None, :]
        outgoing = jnp.dot(
            jnp.transpose(selector).astype(jnp.bfloat16),
            token_rows,
            preferred_element_type=jnp.float32,
        ).astype(jnp.bfloat16)
        outgoing = outgoing.reshape(experts, capacity, 2, half_width)
        arriving = lax.all_to_all(
            lax.all_to_all(outgoing, "ep", split_axis=0, concat_axis=0, tiled=True),
            "sub",
            split_axis=2,
            concat_axis=2,
            tiled=True,
        )
        arriving_rows = arriving.reshape(-1, half_width).astype(jnp.float32)
        running = jnp.dot(arriving_rows, weights_now, precision=lax.Precision.HIGHEST)
        partial_value = running.astype(jnp.bfloat16).reshape(experts, capacity, 2, out_width)
        joined = lax.all_to_all(partial_value, "sub", split_axis=2, concat_axis=2, tiled=True)
        summed = (joined[:, :, 0].astype(jnp.float32) + joined[:, :, 1].astype(jnp.float32)).astype(
            jnp.bfloat16
        )
        returned = lax.all_to_all(summed, "ep", split_axis=0, concat_axis=0, tiled=True)
        weighted = jnp.where(selector, route_weights[step_index].reshape(-1)[:, None], 0.0)
        mixing = jnp.sum(weighted.reshape(token_count, top_count, -1), axis=1)
        combined = jnp.dot(
            mixing,
            returned.reshape(-1, out_width).astype(jnp.float32),
            precision=lax.Precision.HIGHEST,
        )
        results.append(combined.astype(jnp.bfloat16))
    level_output = (new_levels.astype(jnp.float32) * 0.0078125).astype(jnp.bfloat16)[None]
    return (jnp.stack(results), level_output, new_grid[None])


EXTRA_ROWS = 16


def split3(value):
    high = value.astype(jnp.bfloat16)
    rest = value - high.astype(jnp.float32)
    middle = rest.astype(jnp.bfloat16)
    low = (rest - middle.astype(jnp.float32)).astype(jnp.bfloat16)
    return high, middle, low


def raw_levels(weights, step_grid):
    blocks = weights.reshape(step_grid.shape[0], Q_BLOCK, weights.shape[-1])
    nearest = jnp.floor(blocks / step_grid[:, None, :] + 0.5)
    return jnp.clip(nearest, -127.0, 127.0).reshape(weights.shape)


def greet(targets):
    barrier = pltpu.get_barrier_semaphore()
    for target in targets:
        pl.semaphore_signal(
            barrier, inc=1, device_id=target, device_id_type=pl.DeviceIdType.MESH
        )
    pl.semaphore_wait(barrier, len(targets))


def whole_kernel(
    experts,
    arrive_ref,
    active_ref,
    outgoing_ref,
    master_ref,
    stale_ref,
    mixed_ref,
    arrived_ref,
    arriving_ref,
    levels_ref,
    grids_ref,
    pieces_ref,
    spread_refs,
    chosen_refs,
    weights_ref,
    partial_ref,
    other_ref,
    send_one,
    recv_one,
    send_two,
    recv_two,
    send_three,
    recv_three,
    token_send,
    token_recv,
    spread_sems,
    move_sems,
    other_sems,
    one_sems,
    two_sems,
    three_sems,
    local_sem,
):
    me = lax.axis_index("ep")
    core = lax.axis_index("sub")
    steps, _, _, tokens, rows = arriving_ref.shape
    blocks = rows // Q_BLOCK
    width = partial_ref.shape[-1]
    piece_columns = width // experts
    planes = experts // 4
    x = lax.rem(me, 2)
    y = lax.rem(me // 2, 2)
    z = me // 4
    half = width // 2
    MESH = pl.DeviceIdType.MESH
    order = sorted(range(1, experts), key=lambda offset: abs(offset - experts // 2))
    everyone = []
    for offset in range(experts):
        for flip in range(2):
            if offset or flip:
                everyone.append(
                    {"ep": lax.rem(me + offset, experts), "sub": lax.rem(core + flip, 2)}
                )
    own_master = pltpu.make_async_copy(master_ref, weights_ref, local_sem.at[0])
    own_master.start()
    greet(everyone)

    def token_copy(offset, flip):
        target = lax.rem(me + offset, experts)
        side = lax.rem(core + flip, 2)
        columns = pl.ds(pl.multiple_of(side * rows, 128), rows)
        return pltpu.make_async_remote_copy(
            src_ref=outgoing_ref.at[target, :, :, columns],
            dst_ref=arriving_ref.at[:, core, me],
            send_sem=token_send.at[offset, flip],
            recv_sem=token_recv.at[offset, flip],
            device_id={"ep": target, "sub": side},
            device_id_type=MESH,
        )

    token_copies = [
        token_copy(offset, flip) for offset in order + [0] for flip in range(2) if offset or flip
    ]
    for copy in token_copies:
        copy.start()
    own_tokens = pltpu.make_async_copy(
        outgoing_ref.at[me, :, :, pl.ds(pl.multiple_of(core * rows, 128), rows)],
        arriving_ref.at[:, core, me],
        local_sem.at[1],
    )
    own_tokens.start()
    own_master.wait()

    def requantize(piece, carry):
        columns = pl.ds(pl.multiple_of(piece * piece_columns, 128), piece_columns)
        weights = weights_ref[:, columns]
        stale_grid = stale_ref[:, columns]
        new_grid = grid_of(weights)
        new_levels = raw_levels(weights, new_grid)
        stale_levels = raw_levels(weights, stale_grid)
        pieces_ref[piece, 0:rows, :] = (new_levels * 0.0078125).astype(jnp.bfloat16)
        high, middle, low = split3(new_grid)
        fill = jnp.zeros((EXTRA_ROWS - 3 * blocks, piece_columns), jnp.float32)
        parts = [part.astype(jnp.float32) for part in (high, middle, low)]
        extra = jnp.concatenate(parts + [fill], axis=0)
        pieces_ref[piece, rows : rows + EXTRA_ROWS, :] = extra.astype(jnp.bfloat16)
        for step in range(steps):
            moved = active_ref[step : step + 1, :] > 0
            grids_ref[step, 0:blocks, columns] = jnp.where(moved, new_grid, stale_grid)
            levels_ref[step, :, columns] = jnp.where(moved, new_levels, stale_levels).astype(
                jnp.bfloat16
            )
        return carry

    lax.fori_loop(0, experts, requantize, 0)

    cut = rows // 2
    shares = [slice(0, cut), slice(cut, rows + EXTRA_ROWS)]
    spread_copies = []
    for share in range(2):
        copies = []
        for offset in order:
            target = lax.rem(me + offset, experts)
            copy = pltpu.make_async_remote_copy(
                src_ref=pieces_ref.at[target, shares[share]],
                dst_ref=spread_refs[share].at[me],
                send_sem=spread_sems.at[0, share, offset],
                recv_sem=spread_sems.at[1, share, offset],
                device_id={"ep": target, "sub": core},
                device_id_type=MESH,
            )
            copy.start()
            copies.append(copy)
        own_spread = pltpu.make_async_copy(
            pieces_ref.at[me, shares[share]], spread_refs[share].at[me], local_sem.at[2 + share]
        )
        own_spread.start()
        spread_copies.append(copies + [own_spread])

    own_tokens.wait()
    for copy in token_copies:
        copy.wait_recv()

    tile = min(256, width)

    def serve(number, carry):
        columns = pl.ds(pl.multiple_of(number * tile, 128), tile)
        for step in range(steps):
            token_rows = arriving_ref[step].reshape(2 * experts * tokens, rows)
            total = None
            for block in range(blocks):
                here = slice(block * Q_BLOCK, (block + 1) * Q_BLOCK)
                product = jnp.dot(
                    token_rows[:, here],
                    levels_ref[step, here, columns],
                    preferred_element_type=jnp.float32,
                )
                product = product * grids_ref[step, block : block + 1, columns]
                total = product if total is None else total + product
            partial_ref[step, :, :, :, columns] = total.reshape(
                2, experts, tokens, tile
            ).astype(jnp.bfloat16)
        return carry

    sides = [slice(0, half), slice(half, 2 * half)]
    across_x = {"ep": z * 4 + y * 2 + (1 - x), "sub": core}
    across_y = {"ep": z * 4 + (1 - y) * 2 + x, "sub": core}
    other_copies = []
    tiles = half // tile
    for side in range(2):
        lax.fori_loop(side * tiles, (side + 1) * tiles, serve, 0)
        copy = pltpu.make_async_remote_copy(
            src_ref=partial_ref.at[:, 1 - core, :, :, sides[side]],
            dst_ref=other_ref.at[:, :, :, sides[side]],
            send_sem=other_sems.at[0, side],
            recv_sem=other_sems.at[1, side],
            device_id={"ep": me, "sub": 1 - core},
            device_id_type=MESH,
        )
        copy.start()
        other_copies.append(copy)

    def pair(target, side):
        here = sides[side]
        return partial_ref[:, core, target, :, here].astype(jnp.float32) + other_ref[
            :, target, :, here
        ].astype(jnp.float32)

    def send(source, landing, sems, side, device):
        copy = pltpu.make_async_remote_copy(
            src_ref=source.at[side],
            dst_ref=landing.at[side],
            send_sem=sems.at[0, side],
            recv_sem=sems.at[1, side],
            device_id=device,
            device_id_type=MESH,
        )
        copy.start()
        return copy

    one_copies = []
    for side in range(2):
        other_copies[side].wait()

        def first(number, carry, side=side):
            plane, place = number // 2, lax.rem(number, 2)
            if side == 0:
                target = plane * 4 + place * 2 + (1 - x)
            else:
                target = plane * 4 + (1 - y) * 2 + place
            send_one[side, number] = pair(target, side).astype(jnp.bfloat16)
            return carry

        lax.fori_loop(0, 2 * planes, first, 0)
        one_copies.append(
            send(send_one, recv_one, one_sems, side, across_x if side == 0 else across_y)
        )

    columns = pl.ds(pl.multiple_of(me * piece_columns, 128), piece_columns)
    piece_copies = []

    def move(share):
        for copy in spread_copies[share]:
            copy.wait()

        def choose(number, carry):
            chosen_refs[share][number] = spread_refs[share][arrive_ref[number]]
            return carry

        lax.fori_loop(0, experts, choose, 0)
        for offset in order:
            target = lax.rem(me + offset, experts)
            copy = pltpu.make_async_remote_copy(
                src_ref=chosen_refs[share].at[target],
                dst_ref=arrived_ref.at[shares[share], columns],
                send_sem=move_sems.at[0, share, offset],
                recv_sem=move_sems.at[1, share, offset],
                device_id={"ep": target, "sub": core},
                device_id_type=MESH,
            )
            copy.start()
            piece_copies.append(copy)
        own_piece = pltpu.make_async_copy(
            chosen_refs[share].at[me],
            arrived_ref.at[shares[share], columns],
            local_sem.at[4 + share],
        )
        own_piece.start()
        piece_copies.append(own_piece)

    move(0)

    two_copies = []
    for side in range(2):
        one_copies[side].wait()

        def second(plane, carry, side=side):
            if side == 0:
                target, number = plane * 4 + (1 - y) * 2 + x, plane * 2 + (1 - y)
            else:
                target, number = plane * 4 + y * 2 + (1 - x), plane * 2 + (1 - x)
            value = pair(target, side) + recv_one[side, number].astype(jnp.float32)
            send_two[side, plane] = value.astype(jnp.bfloat16)
            return carry

        lax.fori_loop(0, planes, second, 0)
        two_copies.append(
            send(send_two, recv_two, two_sems, side, across_y if side == 0 else across_x)
        )

    def third_value(plane, side):
        target = plane * 4 + y * 2 + x
        number = plane * 2 + (y if side == 0 else x)
        return (
            pair(target, side)
            + recv_one[side, number].astype(jnp.float32)
            + recv_two[side, plane].astype(jnp.float32)
        )

    move(1)

    for side in range(2):
        two_copies[side].wait()
    three_copies = []
    for offset in range(1, planes):
        plane = lax.rem(z + offset, planes)
        for side in range(2):
            send_three[offset - 1, :, :, sides[side]] = third_value(plane, side).astype(
                jnp.bfloat16
            )
        copy = pltpu.make_async_remote_copy(
            src_ref=send_three.at[offset - 1],
            dst_ref=recv_three.at[offset - 1],
            send_sem=three_sems.at[0, offset],
            recv_sem=three_sems.at[1, offset],
            device_id={"ep": plane * 4 + y * 2 + x, "sub": core},
            device_id_type=MESH,
        )
        copy.start()
        three_copies.append(copy)
    for copy in three_copies:
        copy.wait()
    for side in range(2):
        total = third_value(z, side)
        for offset in range(1, planes):
            total = total + recv_three[offset - 1, :, :, sides[side]].astype(jnp.float32)
        mixed_ref[:, :, sides[side]] = total.astype(jnp.bfloat16)
    for copy in piece_copies:
        copy.wait()
    for copy in token_copies:
        copy.wait_send()


def local_small(expert_inputs, routes, route_weights, master, old_steps, move_list):
    experts = lax.axis_size("ep")
    my_index = lax.axis_index("ep")
    steps, tokens, top, inner = expert_inputs.shape
    half, width = master.shape[1:]
    piece_columns = width // experts
    piece_rows = half + EXTRA_ROWS
    any_space = pl.BlockSpec(memory_space=pl.ANY)
    vmem = pl.BlockSpec(memory_space=pltpu.VMEM)
    expert_column, old_column = move_list[:, 0], move_list[:, 1]
    new_column, step_column = move_list[:, 2], move_list[:, 3]
    all_experts = jnp.arange(experts, dtype=jnp.int32)
    old_owner = lookup(expert_column, old_column, all_experts)
    arrive_from = lookup(new_column, old_column, all_experts)
    leave_step = lookup(old_column, step_column, jnp.reshape(my_index, (1,)))[0]
    active = (jnp.arange(steps, dtype=jnp.int32) >= leave_step).astype(jnp.int32)
    active = jnp.broadcast_to(active[:, None], (steps, piece_columns))

    pairs = steps * tokens * top
    ids = routes.reshape(pairs)
    target = jnp.sum(
        jnp.where(ids[:, None] == all_experts[None, :], old_owner[None, :], 0), axis=1
    )
    pair_numbers = jnp.arange(pairs, dtype=jnp.int32)
    slot_numbers = jnp.arange(experts * steps * tokens, dtype=jnp.int32)
    slot = target * (steps * tokens) + pair_numbers // top
    selector = (slot[None, :] == slot_numbers[:, None]).astype(jnp.bfloat16)
    rows = expert_inputs.reshape(pairs, inner).astype(jnp.float32)
    rows = (rows * route_weights.reshape(pairs)[:, None]).astype(jnp.bfloat16)
    outgoing = jnp.dot(selector, rows, preferred_element_type=jnp.float32).astype(jnp.bfloat16)
    outgoing = outgoing.reshape(experts, steps, tokens, inner)

    blocks = half // Q_BLOCK
    planes = experts // 4
    bf16 = jnp.bfloat16
    cuts = [half // 2, half // 2 + EXTRA_ROWS]
    mixed, arrived = pl.pallas_call(
        functools.partial(whole_kernel, experts),
        out_shape=(
            jax.ShapeDtypeStruct((steps, tokens, width), bf16),
            jax.ShapeDtypeStruct((piece_rows, width), bf16),
        ),
        in_specs=[pl.BlockSpec(memory_space=pltpu.SMEM), vmem, any_space, any_space, vmem],
        out_specs=(vmem, vmem),
        scratch_shapes=[
            pltpu.VMEM((steps, 2, experts, tokens, half), bf16),
            pltpu.VMEM((steps, half, width), bf16),
            pltpu.VMEM((steps, max(8, blocks), width), jnp.float32),
            pltpu.VMEM((experts, piece_rows, piece_columns), bf16),
            [pltpu.VMEM((experts, count, piece_columns), bf16) for count in cuts],
            [pltpu.VMEM((experts, count, piece_columns), bf16) for count in cuts],
            pltpu.VMEM((half, width), jnp.float32),
            pltpu.VMEM((steps, 2, experts, tokens, width), bf16),
            pltpu.VMEM((steps, experts, tokens, width), bf16),
            pltpu.VMEM((2, 2 * planes, steps, tokens, width // 2), bf16),
            pltpu.VMEM((2, 2 * planes, steps, tokens, width // 2), bf16),
            pltpu.VMEM((2, planes, steps, tokens, width // 2), bf16),
            pltpu.VMEM((2, planes, steps, tokens, width // 2), bf16),
            pltpu.VMEM((planes - 1, steps, tokens, width), bf16),
            pltpu.VMEM((planes - 1, steps, tokens, width), bf16),
            pltpu.SemaphoreType.DMA((experts, 2)),
            pltpu.SemaphoreType.DMA((experts, 2)),
            pltpu.SemaphoreType.DMA((2, 2, experts)),
            pltpu.SemaphoreType.DMA((2, 2, experts)),
            pltpu.SemaphoreType.DMA((2, 2)),
            pltpu.SemaphoreType.DMA((2, 2)),
            pltpu.SemaphoreType.DMA((2, 2)),
            pltpu.SemaphoreType.DMA((2, planes)),
            pltpu.SemaphoreType.DMA((6,)),
        ],
        compiler_params=pltpu.CompilerParams(
            collective_id=0, has_side_effects=True, vmem_limit_bytes=52 * 1024 * 1024
        ),
    )(arrive_from, active, outgoing, master[0], old_steps[0])
    parts = arrived[half : half + 3 * blocks].astype(jnp.float32).reshape(3, blocks, width)
    new_steps = (parts[0] + parts[1]) + parts[2]
    return mixed, arrived[:half][None], new_steps[None]


def body_for(mesh):
    def body(expert_inputs, routes, route_weights, master, old_steps, move_list):
        experts, cores = mesh.shape["ep"], mesh.shape["sub"]
        tokens, top = routes.shape[1:]
        half, width = master.shape[1:]
        fits = (
            experts % 4 == 0
            and experts <= 16
            and cores == 2
            and tokens % 16 == 0
            and width % (experts * 128) == 0
            and half % Q_BLOCK == 0
            and 3 * (half // Q_BLOCK) <= EXTRA_ROWS
        )
        chosen = local_small if fits else local
        return chosen(expert_inputs, routes, route_weights, master, old_steps, move_list)

    return body


def solution(mesh):
    placed = (
        P(None, ("groups", "ep", "sub"), None, None),
        P(None, ("groups", "ep", "sub"), None),
        P(None, ("groups", "ep", "sub"), None),
        P("ep", "sub", None),
        P("ep", "sub", None),
        P(),
    )
    return jax.shard_map(
        body_for(mesh),
        mesh=mesh,
        in_specs=placed,
        out_specs=(
            P(None, ("groups", "ep", "sub"), None),
            P(("groups", "ep"), "sub", None),
            P(("groups", "ep"), "sub", None),
        ),
        check_vma=False,
    )
```
